768 devices in a mesh: row: 16 (over y, core), col: 48 (over z, x).
Axes of the slice: x: 4, y: 8, z: 12, core: 2. Of those that a mesh axis runs over, the one named last changes fastest.
Arguments:
- panel: bfloat16 [98304, 128], P(('row', 'col')), may hold values from -6 to 6
- previous: bfloat16 [98304, 128], P(('row', 'col')), may hold values from -6 to 6
- blocks: bfloat16 [16, 48, 64, 128, 128], P('row', 'col'), may hold values from -0.046875 to 0.046875
- block_rows: int32 [16, 48, 64], P('row', 'col'), may hold values from 0 to 47
- block_cols: int32 [16, 48, 64], P('row', 'col'), may hold values from 0 to 15
- counts: int32 [16, 48], P('row', 'col'), may hold values from 8 to 64, as said below
- center: float32 [1], replicated, may hold values from -0.5 to 0.5
- half_width: float32 [1], replicated, may hold values from 1 to 2
Outputs:
- filtered: bfloat16 [98304, 128], P(('row', 'col'))
The draws below stay inside these ranges and needn't reach their ends.
Inputs may be any that keep to these rules, and one draw needn't show every extreme that they name: `counts`: live slots of each device; some device has all 64 slots live.
All inputs are finite; a program needn't handle non-finite values.
Results may differ from the reference program's by a relative error of at most 0.014.
Values may be sent and summed in bfloat16 or wider, within the bound.
A program may use at most 32 MiB of HBM per device.

```python
import jax
import jax.numpy as jnp
from jax import lax

BS = 128
K = 128
BPD = 1
BLK_DEV = 64
NROWS = 98304
N_ROW = 16
N_COL = 48


def draw_counts(key, part):
    key = jax.random.fold_in(key, 11)
    drawn = jax.random.randint(key, (N_ROW * N_COL,), BLK_DEV // 8, 3 * BLK_DEV // 4 + 1)
    chosen = jax.random.randint(jax.random.fold_in(key, 1), (), 0, N_ROW * N_COL)
    drawn = jnp.where(jnp.arange(N_ROW * N_COL) == chosen, BLK_DEV, drawn)
    return drawn.reshape(N_ROW, N_COL).astype(jnp.int32)


def place_ends(values, rng, low, high):
    longest = values.shape.index(max(values.shape))
    spots = []
    for shift in (0, 1):
        where = [jax.random.randint(jax.random.fold_in(rng, axis), (), 0, length) for axis, length in enumerate(values.shape)]
        where[longest] = (where[longest] + shift) % values.shape[longest]
        spots.append(tuple(where))
    return values.at[spots[0]].set(low).at[spots[1]].set(high)


def block_scale(rng, dims, cuts, least, largest):
    level, own = 1.0, jax.random.fold_in(rng, 6)
    for position, shards_of in cuts:
        draws = jnp.exp(jax.random.uniform(jax.random.fold_in(own, position), (shards_of,), jnp.float32, least / len(cuts), largest / len(cuts)))
        level = level * jnp.repeat(draws, dims[position] // shards_of).reshape([-1 if axis == position else 1 for axis in range(len(dims))])
    return level


def gaussian(rng, extent, width, limit, split=(), kind=jnp.bfloat16):
    level = block_scale(rng, extent, split, -0.22, 0.18) if split else 1.0
    values = jax.random.normal(rng, extent, jnp.float32) * width * level
    return jnp.minimum(jnp.maximum(values, -limit), limit).astype(kind)


def setup_inputs(seed: int = 0) -> dict:
    arg_keys = jax.random.split(jax.random.key(seed), 9)
    return {
        "panel": gaussian(arg_keys[0], (NROWS, K), 1.0, 6.0, ((0, 768),)),
        "previous": gaussian(arg_keys[1], (NROWS, K), 1.0, 6.0, ((0, 768),)),
        "blocks": gaussian(arg_keys[2], (N_ROW, N_COL, BLK_DEV, BS, BS), (256 * BLK_DEV) ** -0.5, 0.046875, ((0, 16), (1, 48))),
        "block_rows": place_ends(jax.random.randint(arg_keys[3], (N_ROW, N_COL, BLK_DEV), 0, N_COL * BPD), jax.random.fold_in(arg_keys[3], 1), 0, (N_COL * BPD) - 1).astype(jnp.int32),
        "block_cols": place_ends(jax.random.randint(arg_keys[4], (N_ROW, N_COL, BLK_DEV), 0, N_ROW * BPD), jax.random.fold_in(arg_keys[4], 1), 0, (N_ROW * BPD) - 1).astype(jnp.int32),
        "counts": draw_counts(jax.random.fold_in(arg_keys[8], 71), 0),
        "center": jnp.clip(jax.random.uniform(arg_keys[6], (1,), jnp.float32, -0.5, 0.5), -0.5, 0.5),
        "half_width": jnp.clip(jax.random.uniform(arg_keys[7], (1,), jnp.float32, 1.0, 2.0), 1.0, 2.0),
    }


def reference(panel, previous, blocks, block_rows, block_cols, counts, center, half_width):
    total_blocks = N_ROW * N_COL * BPD
    panel_tiles = panel.astype(jnp.float32).reshape(total_blocks, BS, K)
    grid_r = jnp.arange(N_ROW, dtype=jnp.int32)[:, None, None]
    grid_c = jnp.arange(N_COL, dtype=jnp.int32)[None, :, None]
    global_rows = (grid_r * (N_COL * BPD) + block_rows).astype(jnp.int32)
    global_cols = (((block_cols // BPD) * N_COL + grid_c) * BPD + block_cols % BPD).astype(jnp.int32)
    live_mask = (jnp.arange(BLK_DEV, dtype=jnp.int32)[None, None, :] < counts[:, :, None]).astype(jnp.float32)

    def add_row(totals, scan_items):
        stored, rows_here, cols_here, live_here = scan_items
        stored = stored.astype(jnp.float32).reshape(-1, BS, BS)
        rows_here = rows_here.reshape(-1)
        cols_here = cols_here.reshape(-1)
        weight = live_here.reshape(-1, 1, 1)
        direct = jnp.einsum("sab,sbk->sak", stored, panel_tiles[cols_here], precision=lax.Precision.HIGHEST) * weight
        mirror = jnp.einsum("sba,sbk->sak", stored, panel_tiles[rows_here], precision=lax.Precision.HIGHEST) * weight
        totals = totals.at[rows_here].add(direct).at[cols_here].add(mirror)
        return totals, None

    zero_totals = jnp.zeros((total_blocks, BS, K), jnp.float32)
    product, _ = lax.scan(add_row, zero_totals, (blocks, global_rows, global_cols, live_mask))
    product = product.reshape(-1, K)
    result = (2.0 / half_width[0]) * (product - center[0] * panel.astype(jnp.float32)) - previous.astype(jnp.float32)
    return result.astype(jnp.bfloat16)
```

```python
import functools

import jax
import jax.numpy as jnp
from jax import lax
from jax.experimental import pallas as pl
from jax.experimental.pallas import tpu as pltpu
from jax.sharding import PartitionSpec as P

MESH = pl.DeviceIdType.MESH
BF = jnp.bfloat16
F32 = jnp.float32
NX = 4
NR = 3


def kernel(nx, ny, ns, half, tab, center, width, panel, previous, blocks_hbm, out,
           C, G, B, D, M, T, RXA, RZB, RZA, RXB, SA, SB, S3, SH, R3, MS, MR, N, YR,
           bsem, cs, cr, gs, gr, rs, rr, ms, mr):
    row = lax.axis_index("row")
    col = lax.axis_index("col")
    y, k = row // 2, row % 2
    z, x = col // nx, col % nx
    zs, zr = z // NR, z % NR
    nz = ns * NR
    slots = B.shape[0]
    bs = panel.shape[0]
    zm, zp = (zr + NR - 1) % NR, (zr + 1) % NR
    o_ck, o_pr, o_lr, o_pc, o_lc = slots, 2 * slots, 3 * slots, 3 * slots + nz * nx, 4 * slots + nz * nx

    def at(dy=0, dk=0, dz=0, dx=0):
        return {
            "row": ((y + dy) % ny) * 2 + (k + dk) % 2,
            "col": ((z + dz) % nz) * nx + (x + dx) % nx,
        }

    started = []

    def send(src, dst, ssem, rsem, dev):
        cp = pltpu.make_async_remote_copy(
            src_ref=src, dst_ref=dst, send_sem=ssem, recv_sem=rsem, device_id=dev, device_id_type=MESH
        )
        cp.start()
        started.append(cp)

    def got(dst, rsem):
        pltpu.make_async_remote_copy(
            src_ref=dst, dst_ref=dst, send_sem=rsem, recv_sem=rsem, device_id=at(), device_id_type=MESH
        ).wait_recv()

    block_copy = pltpu.make_async_copy(blocks_hbm, B, bsem)
    block_copy.start()

    peers = [at(dk=1)]
    peers += [at(dy=d) for d in range(1, ny)]
    peers += [at(dz=NR * d) for d in range(1, ns)]
    peers += [at(dz=1), at(dz=-1)]
    peers += [at(dx=d) for d in range(1, nx)]
    barrier = pltpu.get_barrier_semaphore()
    for dev in peers:
        pl.semaphore_signal(barrier, inc=1, device_id=dev, device_id_type=MESH)
    own = panel[...]
    C[k * ny + y] = own
    G[zr, zs, x] = own.astype(F32).T.astype(BF)
    D[slots] = jnp.zeros(D.shape[1:], F32)
    M[slots] = jnp.zeros(M.shape[1:], F32)
    pl.semaphore_wait(barrier, len(peers))

    for d in range(1, ny):
        send(C.at[k * ny + y], C.at[k * ny + y], cs.at[d], cr.at[d], at(dy=d))
    send(C.at[k * ny + y], C.at[k * ny + y], cs.at[0], cr.at[0], at(dk=1))
    for d in range(1, ns):
        send(G.at[zr, zs, x], G.at[zr, zs, x], gs.at[0, d], gr.at[0, d], at(dz=NR * d))
    for d in range(1, ns):
        got(G.at[zr, zs, x], gr.at[0, d])
    for e, dz in enumerate((1, -1)):
        send(G.at[zr, :, x], G.at[zr, :, x], gs.at[1, e], gr.at[1, e], at(dz=dz))
    for d in range(1, nx):
        send(G.at[zr, :, x], G.at[zr, :, x], gs.at[2, d], gr.at[2, d], at(dx=d))

    for d in range(1, ny):
        got(C.at[k * ny + y], cr.at[d])
        there = C.at[k * ny + (y + ny - d) % ny]
        send(there, there, cs.at[ny + d], cr.at[ny + d], at(dk=1))

    for e, q in enumerate((zm, zp)):
        got(G.at[zr, :, x], gr.at[1, e])
        for d in range(1, nx):
            part = G.at[q, :, x, pl.ds(0, half)]
            send(part, part, gs.at[3 + e, d], gr.at[3 + e, d], at(dx=d))
    for d in range(1, nx):
        got(G.at[zr, :, x], gr.at[2, d])
        for e, dz in enumerate((1, -1)):
            part = G.at[zr, :, (x + nx - d) % nx, pl.ds(half, bs - half)]
            send(part, part, gs.at[5 + e, d], gr.at[5 + e, d], at(dz=dz))

    block_copy.wait()
    got(C.at[k * ny + y], cr.at[0])
    for d in range(1, ny):
        got(C.at[k * ny + y], cr.at[ny + d])

    def direct(s, carry):
        p = C[tab[o_ck + s]]
        D[s] = jnp.dot(B[s], p, preferred_element_type=F32) + D[tab[o_pr + s]]
        return carry

    lax.fori_loop(0, slots, direct, 0, unroll=8)

    def round_rows(i, carry):
        T[i // (ns * nx), (i // nx) % ns, i % nx] = D[tab[o_lr + i]].astype(BF)
        return carry

    lax.fori_loop(0, nz * nx, round_rows, 0, unroll=4)
    for d in range(1, nx):
        send(T.at[:, :, (x + d) % nx, pl.ds(0, half)], RXA.at[d - 1], rs.at[0, d], rr.at[0, d], at(dx=d))
    for e, (q, dz) in enumerate(((zp, 1), (zm, -1))):
        send(T.at[q, :, :, pl.ds(half, bs - half)], RZB.at[e], rs.at[1, e], rr.at[1, e], at(dz=dz))

    for e in range(2):
        for d in range(1, nx):
            got(G.at[zr, :, x, pl.ds(0, half)], gr.at[3 + e, d])
            got(G.at[zr, :, x, pl.ds(half, bs - half)], gr.at[5 + e, d])

    def mirror(s, carry):
        t = tab[s]
        p = G[lax.div(t, ns * nx), lax.rem(lax.div(t, nx), ns), lax.rem(t, nx)]
        M[s] = jnp.dot(p, B[s], preferred_element_type=F32) + M[tab[o_pc + s]]
        return carry

    lax.fori_loop(0, slots, mirror, 0, unroll=8)

    def round_other(i, carry):
        MS[i] = M[tab[o_lc + (1 - k) * ny + i]].astype(BF)
        return carry

    lax.fori_loop(0, ny, round_other, 0, unroll=4)
    send(MS, MR, ms.at[0], mr.at[0], at(dk=1))

    for e in range(2):
        got(RZB.at[e], rr.at[1, e])

    def sum_b(i, carry):
        s, w = i // nx, i % nx
        total = D[tab[o_lr + (zr * ns + s) * nx + w]][half:]
        total = total + RZB[0, s, w].astype(F32) + RZB[1, s, w].astype(F32)
        SB[w, s] = total.astype(BF)
        return carry

    lax.fori_loop(0, ns * nx, sum_b, 0, unroll=4)
    for d in range(1, nx):
        send(SB.at[(x + d) % nx], RXB.at[d - 1], rs.at[2, d], rr.at[2, d], at(dx=d))
    for d in range(1, nx):
        got(RXA.at[d - 1], rr.at[0, d])

    def sum_a(i, carry):
        q, s = i // ns, i % ns
        total = D[tab[o_lr + i * nx + x]][:half]
        for d in range(1, nx):
            total = total + RXA[d - 1, q, s].astype(F32)
        SA[q, s] = total.astype(BF)
        return carry

    lax.fori_loop(0, NR * ns, sum_a, 0, unroll=4)
    for e, (q, dz) in enumerate(((zp, 1), (zm, -1))):
        send(SA.at[q], RZA.at[e], rs.at[3, e], rr.at[3, e], at(dz=dz))

    got(MR, mr.at[0])

    def sum_m(i, carry):
        N[i] = (M[tab[o_lc + k * ny + i]] + MR[i].astype(F32)).astype(BF)
        return carry

    lax.fori_loop(0, ny, sum_m, 0, unroll=4)
    for d in range(1, ny):
        send(N.at[(y + d) % ny], YR.at[d - 1], ms.at[d], mr.at[d], at(dy=d))

    for e in range(2):
        got(RZA.at[e], rr.at[3, e])
    for d in range(1, nx):
        got(RXB.at[d - 1], rr.at[2, d])

    def sum_3(s, carry):
        a = SA[zr, s].astype(F32) + RZA[0, s].astype(F32) + RZA[1, s].astype(F32)
        b = SB[x, s].astype(F32)
        for d in range(1, nx):
            b = b + RXB[d - 1, s].astype(F32)
        S3[s, :half] = a
        S3[s, half:] = b
        SH[s, :half] = a.astype(BF)
        SH[s, half:] = b.astype(BF)
        return carry

    lax.fori_loop(0, ns, sum_3, 0, unroll=ns)
    for d in range(1, ns):
        send(SH.at[(zs + d) % ns], R3.at[d - 1], rs.at[4, d], rr.at[4, d], at(dz=NR * d))

    total = M[tab[o_lc + k * ny + y]] + MR[y].astype(F32)
    for d in range(1, ny):
        got(YR.at[d - 1], mr.at[d])
        total = total + YR[d - 1].astype(F32)
    product = total.T + S3[zs]
    scale = 2.0 / jnp.full((bs, bs), width[0], F32)
    shift = center[0] * panel[...].astype(F32)
    before = previous[...].astype(F32)
    for d in range(1, ns):
        got(R3.at[d - 1], rr.at[4, d])
        product = product + R3[d - 1].astype(F32)
    out[...] = (scale * (product - shift) - before).astype(BF)
    for cp in started:
        cp.wait_send()


def body(nx, panel, previous, blocks, block_rows, block_cols, counts, center, half_width):
    bs = panel.shape[0]
    ny = lax.axis_size("row") // 2
    ncol = lax.axis_size("col")
    nz = ncol // nx
    ns = nz // NR
    slots = blocks.shape[2]
    half = bs // 2
    rows = block_rows.reshape(slots)
    cols = block_cols.reshape(slots)
    count = counts.reshape(())
    zi = rows // nx
    rk = ((zi % NR) * ns + zi // NR) * nx + rows % nx
    ck = (cols % 2) * ny + cols // 2
    place = jnp.arange(slots, dtype=jnp.int32)
    full = jnp.broadcast_to(count, (ncol,))
    want = jnp.concatenate([rk, jnp.arange(ncol, dtype=jnp.int32), ck, jnp.arange(2 * ny, dtype=jnp.int32)])
    limit = jnp.concatenate([place, full, place, full[: 1].repeat(2 * ny)])
    is_row = jnp.arange(want.shape[0]) < slots + ncol
    keys = jnp.where(is_row[:, None], rk[None, :], ck[None, :])
    hit = (keys == want[:, None]) & (place[None, :] < limit[:, None])
    found = jnp.max(jnp.where(hit, place[None, :], -1), axis=1)
    found = jnp.where(found < 0, slots, found)
    tab = jnp.concatenate([rk, ck, found])

    smem = pl.BlockSpec(memory_space=pltpu.SMEM)
    vmem = pl.BlockSpec(memory_space=pltpu.VMEM)
    dma = pltpu.SemaphoreType.DMA
    rest = bs - half
    return pl.pallas_call(
        functools.partial(kernel, nx, ny, ns, half),
        name="filter_step",
        out_shape=jax.ShapeDtypeStruct((bs, bs), BF),
        in_specs=[smem, smem, smem, vmem, vmem, pl.BlockSpec(memory_space=pl.ANY)],
        out_specs=vmem,
        scratch_shapes=[
            pltpu.VMEM((2 * ny, bs, bs), BF),
            pltpu.VMEM((NR, ns, nx, bs, bs), BF),
            pltpu.VMEM((slots, bs, bs), BF),
            pltpu.VMEM((slots + 1, bs, bs), F32),
            pltpu.VMEM((slots + 1, bs, bs), F32),
            pltpu.VMEM((NR, ns, nx, bs, bs), BF),
            pltpu.VMEM((nx - 1, NR, ns, half, bs), BF),
            pltpu.VMEM((2, ns, nx, rest, bs), BF),
            pltpu.VMEM((2, ns, half, bs), BF),
            pltpu.VMEM((nx - 1, ns, rest, bs), BF),
            pltpu.VMEM((NR, ns, half, bs), BF),
            pltpu.VMEM((nx, ns, rest, bs), BF),
            pltpu.VMEM((ns, bs, bs), F32),
            pltpu.VMEM((ns, bs, bs), BF),
            pltpu.VMEM((max(ns - 1, 1), bs, bs), BF),
            pltpu.VMEM((ny, bs, bs), BF),
            pltpu.VMEM((ny, bs, bs), BF),
            pltpu.VMEM((ny, bs, bs), BF),
            pltpu.VMEM((ny - 1, bs, bs), BF),
            dma,
            dma((2 * ny,)), dma((2 * ny,)),
            dma((7, 4)), dma((7, 4)),
            dma((5, 4)), dma((5, 4)),
            dma((ny,)), dma((ny,)),
        ],
        compiler_params=pltpu.CompilerParams(
            collective_id=0, has_side_effects=True, vmem_limit_bytes=48 << 20
        ),
    )(tab, center, half_width, panel, previous, blocks.reshape(slots, bs, bs))


def solution(mesh):
    placed = (
        P(("row", "col"), None),
        P(("row", "col"), None),
        P("row", "col", None, None, None),
        P("row", "col", None),
        P("row", "col", None),
        P("row", "col"),
        P(),
        P(),
    )
    return jax.shard_map(
        functools.partial(body, NX), mesh=mesh, in_specs=placed, out_specs=P(("row", "col"), None), check_vma=False
    )
```

```python
import functools

import jax
import jax.numpy as jnp
from jax import lax
from jax.experimental import pallas as pl
from jax.experimental.pallas import tpu as pltpu
from jax.sharding import PartitionSpec as P

MESH = pl.DeviceIdType.MESH
BF = jnp.bfloat16
F32 = jnp.float32
I32 = jnp.int32
NX = 4
NR = 3
GATHER_ROWS = 64
REDUCE_ROWS = 48
UNROLL = 32


class Lane:
    def __init__(self, sends, recvs):
        self.sends, self.recvs, self.count, self.started = sends, recvs, 0, []

    def make(self, src, dst, dev):
        i, self.count = self.count, self.count + 1
        cp = pltpu.make_async_remote_copy(
            src_ref=src, dst_ref=dst, send_sem=self.sends.at[i], recv_sem=self.recvs.at[i],
            device_id=dev, device_id_type=MESH,
        )
        self.started.append(cp)
        return i, cp

    def send(self, src, dst, dev):
        i, cp = self.make(src, dst, dev)
        cp.start()
        return i

    def got(self, like, i, dev):
        pltpu.make_async_remote_copy(
            src_ref=like, dst_ref=like, send_sem=self.recvs.at[i], recv_sem=self.recvs.at[i],
            device_id=dev, device_id_type=MESH,
        ).wait_recv()

    def drain(self):
        for cp in self.started:
            cp.wait_send()


def kernel(nx, ny, ns, count, center, width, panel_hbm, previous_hbm, blocks_hbm, rows_hbm, cols_hbm, out,
           panel, previous, B, rows, cols, tabv, tab,
           C, G, D, M, T, RXA, RZB, RZA, RXB, SA, SB, S3, SH, R3, MS, MR, N, YR,
           lsem, cs, cr, gs, gr, rs, rr, ms, mr):
    row = lax.axis_index("row")
    col = lax.axis_index("col")
    y, k = row // 2, row % 2
    z, x = col // nx, col % nx
    zs, zr = z // NR, z % NR
    nz = ns * NR
    h = ns // 2
    par, pair = zs % 2, zs // 2
    slot = par * h + pair
    slots = B.shape[0]
    bs = panel.shape[0]
    zm, zp = (zr + NR - 1) % NR, (zr + 1) % NR
    ga, ra = GATHER_ROWS, REDUCE_ROWS
    lo, hi = pl.ds(0, ga), pl.ds(ga, bs - ga)
    rlo, rhi = pl.ds(0, ra), pl.ds(ra, bs - ra)
    ly, lg, lr, lm = Lane(cs, cr), Lane(gs, gr), Lane(rs, rr), Lane(ms, mr)

    def at(dy=0, dk=0, dz=0, dx=0):
        return {
            "row": ((y + dy) % ny) * 2 + (k + dk) % 2,
            "col": ((z + dz) % nz) * nx + (x + dx) % nx,
        }

    here = at()
    loads = [
        pltpu.make_async_copy(a, b, lsem.at[i])
        for i, (a, b) in enumerate([
            (panel_hbm, panel), (rows_hbm, rows), (cols_hbm, cols), (blocks_hbm, B), (previous_hbm, previous),
        ])
    ]
    loads[0].start()
    peers = [at(dk=1)]
    peers += [at(dy=d) for d in range(1, ny)]
    peers += [at(dz=NR * d) for d in range(1, ns)]
    peers += [at(dz=1), at(dz=-1)]
    peers += [at(dx=d) for d in range(1, nx)]
    barrier = pltpu.get_barrier_semaphore()
    for dev in peers:
        pl.semaphore_signal(barrier, inc=1, device_id=dev, device_id_type=MESH)
    for cp in loads[1:]:
        cp.start()
    loads[0].wait()
    own = panel[...]
    mine = C.at[k * ny + y]
    C[k * ny + y] = own
    G[zr, slot, x] = own.astype(F32).T.astype(BF)
    pl.semaphore_wait(barrier, len(peers))

    ownt = G.at[zr, slot, x]
    first = {d: lg.send(ownt, ownt, at(dz=NR * d)) for d in range(1, ns, 2)}
    for d in range(1, ny):
        ly.send(mine, mine, at(dy=d))
    ly.send(mine, mine, at(dk=1))

    def spread(piece):
        return (
            [lg.send(piece, piece, at(dz=dz)) for dz in (1, -1)],
            [lg.send(piece, piece, at(dx=d)) for d in range(1, nx)],
        )

    near = [spread(ownt)]
    first.update({d: lg.send(ownt, ownt, at(dz=NR * d)) for d in range(2, ns, 2)})

    D[slots] = jnp.zeros(D.shape[1:], F32)
    M[slots] = jnp.zeros(M.shape[1:], F32)
    tabv[...] = jnp.zeros(tabv.shape, I32)
    for cp in loads[1:3]:
        cp.wait()
    shift = nx.bit_length() - 1
    r = rows[...]
    rz = lax.shift_right_logical(r, shift)
    rzs = lax.shift_right_logical(rz * 11, 5)
    rk = (rz - rzs * NR) * ns + (rzs & 1) * h + lax.shift_right_logical(rzs, 1)
    rk = rk * nx + (r & (nx - 1))
    c = cols[...]
    ck = (c & 1) * ny + lax.shift_right_logical(c, 1)
    square = (slots, slots)
    t_of = lax.broadcasted_iota(I32, square, 0)
    s_of = lax.broadcasted_iota(I32, square, 1)
    alive = t_of < count[0, 0]
    tabv[0:1, 0:slots] = rk
    tabv[1:2, 0:slots] = ck
    for i, key in ((2, rk), (4, ck)):
        wide = jnp.broadcast_to(key, square)
        tall = wide.T
        before = jnp.max(jnp.where((tall == wide) & (t_of < s_of), t_of, -1), axis=0, keepdims=True)
        last = jnp.max(jnp.where((tall == s_of) & alive, t_of, -1), axis=0, keepdims=True)
        tabv[i : i + 1, 0:slots] = jnp.where(before < 0, slots, before)
        tabv[i + 1 : i + 2, 0:slots] = jnp.where(last < 0, slots, last)
    table_copy = pltpu.make_async_copy(tabv, tab, lsem.at[5])
    table_copy.start()

    for d in range(1, ns, 2):
        lg.got(ownt, first[d], here)
    near.append(spread(G.at[zr, pl.ds((1 - par) * h, h), x]))

    def slots_of(source, kind):
        szs = source // NR
        spar, spair = szs % 2, szs // 2
        start = (spar * h + spair, (1 - spar) * h, spar * h + 1 - spair)[kind]
        return pl.ds(start, h if kind == 1 else 1)

    corner = []

    def corners(kind):
        like = G.at[zr, slots_of(z, kind), x]
        for e, dz in enumerate((1, -1)):
            lg.got(like, near[kind][0][e], here)
            source = (z + nz - dz) % nz
            part = G.at[source % NR, slots_of(source, kind), x, lo]
            for d in range(1, nx):
                corner.append((part, lg.send(part, part, at(dx=d))))
        for d in range(1, nx):
            lg.got(like, near[kind][1][d - 1], here)
            part = G.at[zr, slots_of(z, kind), (x + nx - d) % nx, hi]
            for dz in (1, -1):
                corner.append((part, lg.send(part, part, at(dz=dz))))

    corners(0)
    if ns > 2:
        for d in range(2, ns, 2):
            lg.got(ownt, first[d], here)
        near.append(spread(G.at[zr, slots_of(z, 2), x]))

    for d in range(1, ny):
        ly.got(mine, d - 1, here)
        there = C.at[k * ny + (y + ny - d) % ny]
        ly.send(there, there, at(dk=1))
    corners(1)

    table_copy.wait()
    loads[3].wait()
    for i in range(ny - 1, 2 * ny - 1):
        ly.got(mine, i, here)

    def direct(s, carry):
        D[s] = jnp.dot(B[s], C[tab[1, s]], preferred_element_type=F32) + D[tab[2, s]]
        return carry

    lax.fori_loop(0, slots, direct, 0, unroll=UNROLL)

    def round_rows(i, carry):
        T[i // (ns * nx), (i // nx) % ns, i % nx] = D[tab[3, i]].astype(BF)
        return carry

    lax.fori_loop(0, nz * nx, round_rows, 0, unroll=8)
    if ns > 2:
        corners(2)
    stage = []
    for p in range(2):
        part = pl.ds(p * h, h)
        stage.append((
            [lr.send(T.at[:, part, (x + d) % nx, rlo], RXA.at[d - 1, :, part], at(dx=d)) for d in range(1, nx)],
            [
                lr.send(T.at[q, part, :, rhi], RZB.at[e, part], at(dz=dz))
                for e, (q, dz) in enumerate(((zp, 1), (zm, -1)))
            ],
        ))

    for like, i in corner:
        lg.got(like, i, here)

    def mirror(s, carry):
        t = tab[0, s]
        p = G[lax.div(t, ns * nx), lax.rem(lax.div(t, nx), ns), lax.rem(t, nx)]
        M[s] = jnp.dot(p, B[s], preferred_element_type=F32) + M[tab[4, s]]
        return carry

    lax.fori_loop(0, slots, mirror, 0, unroll=UNROLL)

    def round_other(i, carry):
        MS[i] = M[tab[5, (1 - k) * ny + i]].astype(BF)
        return carry

    lax.fori_loop(0, ny, round_other, 0, unroll=8)
    swap = lm.send(MS, MR, at(dk=1))

    second = []

    def sums(p):
        part = pl.ds(p * h, h)
        for e in range(2):
            lr.got(RZB.at[e, part], stage[p][1][e], here)

        def sum_b(i, carry):
            s, w = p * h + i // nx, i % nx
            total = D[tab[3, (zr * ns + s) * nx + w]][ra:]
            total = total + RZB[0, s, w].astype(F32) + RZB[1, s, w].astype(F32)
            SB[w, s] = total.astype(BF)
            return carry

        lax.fori_loop(0, h * nx, sum_b, 0, unroll=4)
        over_x = [lr.send(SB.at[(x + d) % nx, part], RXB.at[d - 1, part], at(dx=d)) for d in range(1, nx)]
        for d in range(1, nx):
            lr.got(RXA.at[d - 1, :, part], stage[p][0][d - 1], here)

        def sum_a(i, carry):
            q, s = i // h, p * h + i % h
            total = D[tab[3, (q * ns + s) * nx + x]][:ra]
            for d in range(1, nx):
                total = total + RXA[d - 1, q, s].astype(F32)
            SA[q, s] = total.astype(BF)
            return carry

        lax.fori_loop(0, NR * h, sum_a, 0, unroll=NR)
        over_z = [
            lr.send(SA.at[q, part], RZA.at[e, part], at(dz=dz)) for e, (q, dz) in enumerate(((zp, 1), (zm, -1)))
        ]
        second.append((over_x, over_z))

    sums(0)

    lm.got(MR, swap, here)

    def sum_m(i, carry):
        N[i] = (M[tab[5, k * ny + i]] + MR[i].astype(F32)).astype(BF)
        return carry

    lax.fori_loop(0, ny, sum_m, 0, unroll=8)
    over_y = [lm.send(N.at[(y + d) % ny], YR.at[d - 1], at(dy=d)) for d in range(1, ny)]
    sums(1)

    third = []
    for d in range(1, ns):
        to = (zs + d) % ns
        third.append((to, *lr.make(SH.at[(to % 2) * h + to // 2], R3.at[d - 1], at(dz=NR * d))))
    for p in range(2):
        part = pl.ds(p * h, h)
        over_x, over_z = second[p]
        for e in range(2):
            lr.got(RZA.at[e, part], over_z[e], here)
        for d in range(1, nx):
            lr.got(RXB.at[d - 1, part], over_x[d - 1], here)
        for j in range(h):
            s = p * h + j
            a = SA[zr, s].astype(F32) + RZA[0, s].astype(F32) + RZA[1, s].astype(F32)
            b = SB[x, s].astype(F32)
            for d in range(1, nx):
                b = b + RXB[d - 1, s].astype(F32)
            S3[s, :ra] = a
            S3[s, ra:] = b
            SH[s, :ra] = a.astype(BF)
            SH[s, ra:] = b.astype(BF)
        for to, _, cp in third:
            pl.when(to % 2 == p)(cp.start)

    total = M[tab[5, k * ny + y]] + MR[y].astype(F32)
    for d in range(1, ny):
        lm.got(YR.at[d - 1], over_y[d - 1], here)
        total = total + YR[d - 1].astype(F32)
    for cp in loads[4:]:
        cp.wait()
    product = total.T + S3[slot]
    scale = 2.0 / jnp.full((bs, bs), width[0], F32)
    moved = center[0] * panel[...].astype(F32)
    before = previous[...].astype(F32)
    for d in range(1, ns):
        lr.got(R3.at[d - 1], third[d - 1][1], here)
        product = product + R3[d - 1].astype(F32)
    out[...] = (scale * (product - moved) - before).astype(BF)
    for lane in (ly, lg, lr, lm):
        lane.drain()


def body(nx, panel, previous, blocks, block_rows, block_cols, counts, center, half_width):
    bs = panel.shape[0]
    ny = lax.axis_size("row") // 2
    ns = lax.axis_size("col") // nx // NR
    slots = blocks.shape[2]
    ra, rb = REDUCE_ROWS, bs - REDUCE_ROWS
    hbm = pl.BlockSpec(memory_space=pltpu.HBM)
    dma = pltpu.SemaphoreType.DMA
    vmem = pltpu.VMEM
    gathers = (ns - 1) + min(ns, 3) * (nx + 1 + 4 * (nx - 1))
    reduces = 4 * (nx + 1) + ns - 1
    return pl.pallas_call(
        functools.partial(kernel, nx, ny, ns),
        name="filter_step",
        out_shape=jax.ShapeDtypeStruct((bs, bs), BF),
        in_specs=[pl.BlockSpec(memory_space=pltpu.SMEM)] * 3 + [hbm] * 5,
        out_specs=pl.BlockSpec(memory_space=pltpu.VMEM),
        scratch_shapes=[
            vmem((bs, bs), BF),
            vmem((bs, bs), BF),
            vmem((slots, bs, bs), BF),
            vmem((1, slots), I32),
            vmem((1, slots), I32),
            vmem((8, 128), I32),
            pltpu.SMEM((8, 128), I32),
            vmem((2 * ny, bs, bs), BF),
            vmem((NR, ns, nx, bs, bs), BF),
            vmem((slots + 1, bs, bs), F32),
            vmem((slots + 1, bs, bs), F32),
            vmem((NR, ns, nx, bs, bs), BF),
            vmem((nx - 1, NR, ns, ra, bs), BF),
            vmem((2, ns, nx, rb, bs), BF),
            vmem((2, ns, ra, bs), BF),
            vmem((nx - 1, ns, rb, bs), BF),
            vmem((NR, ns, ra, bs), BF),
            vmem((nx, ns, rb, bs), BF),
            vmem((ns, bs, bs), F32),
            vmem((ns, bs, bs), BF),
            vmem((ns - 1, bs, bs), BF),
            vmem((ny, bs, bs), BF),
            vmem((ny, bs, bs), BF),
            vmem((ny, bs, bs), BF),
            vmem((ny - 1, bs, bs), BF),
            dma((6,)),
            dma((2 * ny - 1,)), dma((2 * ny - 1,)),
            dma((gathers,)), dma((gathers,)),
            dma((reduces,)), dma((reduces,)),
            dma((ny,)), dma((ny,)),
        ],
        compiler_params=pltpu.CompilerParams(
            collective_id=0, has_side_effects=True, vmem_limit_bytes=60 << 20
        ),
    )(
        counts, center, half_width, panel, previous, blocks.reshape(slots, bs, bs),
        block_rows.reshape(1, slots), block_cols.reshape(1, slots),
    )


def solution(mesh):
    placed = (
        P(("row", "col"), None),
        P(("row", "col"), None),
        P("row", "col", None, None, None),
        P("row", "col", None),
        P("row", "col", None),
        P("row", "col"),
        P(),
        P(),
    )
    return jax.shard_map(
        functools.partial(body, NX), mesh=mesh, in_specs=placed, out_specs=P(("row", "col"), None), check_vma=False
    )
```

```python
import functools

import jax
import jax.numpy as jnp
from jax import lax
from jax.experimental import pallas as pl
from jax.experimental.pallas import tpu as pltpu
from jax.sharding import PartitionSpec as P

MESH = pl.DeviceIdType.MESH
BF = jnp.bfloat16
F32 = jnp.float32
I32 = jnp.int32
NX = 4
NR = 3
GATHER_ROWS = 64
PIECES = ((16, 32), (16, 32), (16, 16))
UNROLL = 32


class Lane:
    def __init__(self, sends, recvs):
        self.sends, self.recvs, self.count, self.started = sends, recvs, 0, []

    def make(self, src, dst, dev):
        i, self.count = self.count, self.count + 1
        cp = pltpu.make_async_remote_copy(
            src_ref=src, dst_ref=dst, send_sem=self.sends.at[i], recv_sem=self.recvs.at[i],
            device_id=dev, device_id_type=MESH,
        )
        self.started.append(cp)
        return i, cp

    def send(self, src, dst, dev):
        i, cp = self.make(src, dst, dev)
        cp.start()
        return i

    def got(self, like, i, dev):
        pltpu.make_async_remote_copy(
            src_ref=like, dst_ref=like, send_sem=self.recvs.at[i], recv_sem=self.recvs.at[i],
            device_id=dev, device_id_type=MESH,
        ).wait_recv()

    def drain(self):
        for cp in self.started:
            cp.wait_send()


def kernel(nx, ny, ns, count, center, width, panel_hbm, previous_hbm, blocks_hbm, rows_hbm, cols_hbm, out,
           panel, previous, B, rows, cols, tabv, tab,
           C, G, D, M, T, RXA, RZB, RZA, RXB, SA, SB, S3, SH, R3, MS, MR, N, YR,
           lsem, cs, cr, gs, gr, rs, rr, ms, mr):
    row = lax.axis_index("row")
    col = lax.axis_index("col")
    y, k = row // 2, row % 2
    z, x = col // nx, col % nx
    zs, zr = z // NR, z % NR
    nz = ns * NR
    h = ns // 2
    par, pair = zs % 2, zs // 2
    slot = par * h + pair
    place = lambda zs: (zs % 2) * h + zs // 2
    slots = B.shape[0]
    bs = panel.shape[0]
    zm, zp = (zr + NR - 1) % NR, (zr + 1) % NR
    lo, hi = pl.ds(0, GATHER_ROWS), pl.ds(GATHER_ROWS, bs - GATHER_ROWS)
    spans, start = [], 0
    for a, b in PIECES:
        spans.append((pl.ds(start, a), pl.ds(start + a, b), pl.ds(start, a + b)))
        start += a + b
    ly, lg, lr, lm = Lane(cs, cr), Lane(gs, gr), Lane(rs, rr), Lane(ms, mr)

    def at(dy=0, dk=0, dz=0, dx=0):
        return {
            "row": ((y + dy) % ny) * 2 + (k + dk) % 2,
            "col": ((z + dz) % nz) * nx + (x + dx) % nx,
        }

    here = at()
    loads = [
        pltpu.make_async_copy(a, b, lsem.at[i])
        for i, (a, b) in enumerate([
            (panel_hbm, panel), (rows_hbm, rows), (cols_hbm, cols), (blocks_hbm, B), (previous_hbm, previous),
        ])
    ]
    loads[0].start()
    peers = [at(dk=1)]
    peers += [at(dy=d) for d in range(1, ny)]
    peers += [at(dz=NR * d) for d in range(1, ns)]
    peers += [at(dz=1), at(dz=-1)]
    peers += [at(dx=d) for d in range(1, nx)]
    barrier = pltpu.get_barrier_semaphore()
    for dev in peers:
        pl.semaphore_signal(barrier, inc=1, device_id=dev, device_id_type=MESH)
    for cp in loads[1:]:
        cp.start()
    loads[0].wait()
    own = panel[...]
    mine = C.at[k * ny + y]
    C[k * ny + y] = own
    G[zr, slot, x] = own.astype(F32).T.astype(BF)
    pl.semaphore_wait(barrier, len(peers))

    ownt = G.at[zr, slot, x]
    first = {d: lg.send(ownt, ownt, at(dz=NR * d)) for d in range(1, ns, 2)}

    def spread(piece):
        return (
            [lg.send(piece, piece, at(dz=dz)) for dz in (1, -1)],
            [lg.send(piece, piece, at(dx=d)) for d in range(1, nx)],
        )

    near = [spread(ownt)]
    first.update({d: lg.send(ownt, ownt, at(dz=NR * d)) for d in range(2, ns, 2)})
    for d in range(1, ny):
        ly.send(mine, mine, at(dy=d))
    ly.send(mine, mine, at(dk=1))

    D[slots] = jnp.zeros(D.shape[1:], F32)
    M[slots] = jnp.zeros(M.shape[1:], F32)
    tabv[...] = jnp.zeros(tabv.shape, I32)
    for cp in loads[1:3]:
        cp.wait()
    shift = nx.bit_length() - 1
    r = rows[...]
    rz = lax.shift_right_logical(r, shift)
    rzs = lax.shift_right_logical(rz * 11, 5)
    rk = (rz - rzs * NR) * ns + (rzs & 1) * h + lax.shift_right_logical(rzs, 1)
    rk = rk * nx + (r & (nx - 1))
    c = cols[...]
    ck = (c & 1) * ny + lax.shift_right_logical(c, 1)
    square = (slots, slots)
    t_of = lax.broadcasted_iota(I32, square, 0)
    s_of = lax.broadcasted_iota(I32, square, 1)
    alive = t_of < count[0, 0]
    tabv[0:1, 0:slots] = rk
    tabv[1:2, 0:slots] = ck
    for i, key in ((2, rk), (4, ck)):
        wide = jnp.broadcast_to(key, square)
        tall = wide.T
        before = jnp.max(jnp.where((tall == wide) & (t_of < s_of), t_of, -1), axis=0, keepdims=True)
        last = jnp.max(jnp.where((tall == s_of) & alive, t_of, -1), axis=0, keepdims=True)
        tabv[i : i + 1, 0:slots] = jnp.where(before < 0, slots, before)
        tabv[i + 1 : i + 2, 0:slots] = jnp.where(last < 0, slots, last)
    table_copy = pltpu.make_async_copy(tabv, tab, lsem.at[5])
    table_copy.start()

    for d in range(1, ns, 2):
        lg.got(ownt, first[d], here)
    near.append(spread(G.at[zr, pl.ds((1 - par) * h, h), x]))

    def slots_of(source, kind):
        szs = source // NR
        spar, spair = szs % 2, szs // 2
        start = (spar * h + spair, (1 - spar) * h, spar * h + 1 - spair)[kind]
        return pl.ds(start, h if kind == 1 else 1)

    corner = []

    def corners(kind):
        like = G.at[zr, slots_of(z, kind), x]
        for e, dz in enumerate((1, -1)):
            lg.got(like, near[kind][0][e], here)
            source = (z + nz - dz) % nz
            part = G.at[source % NR, slots_of(source, kind), x, lo]
            for d in range(1, nx):
                corner.append((part, lg.send(part, part, at(dx=d))))
        for d in range(1, nx):
            lg.got(like, near[kind][1][d - 1], here)
            part = G.at[zr, slots_of(z, kind), (x + nx - d) % nx, hi]
            for dz in (1, -1):
                corner.append((part, lg.send(part, part, at(dz=dz))))

    corners(0)
    if ns > 2:
        for d in range(2, ns, 2):
            lg.got(ownt, first[d], here)
        near.append(spread(G.at[zr, slots_of(z, 2), x]))

    for d in range(1, ny):
        ly.got(mine, d - 1, here)
        there = C.at[k * ny + (y + ny - d) % ny]
        ly.send(there, there, at(dk=1))
    corners(1)

    table_copy.wait()
    loads[3].wait()
    for i in range(ny - 1, 2 * ny - 1):
        ly.got(mine, i, here)

    def direct(s, carry):
        D[s] = jnp.dot(B[s], C[tab[1, s]], preferred_element_type=F32) + D[tab[2, s]]
        return carry

    lax.fori_loop(0, slots, direct, 0, unroll=UNROLL)

    if ns > 2:
        corners(2)
    stage = []
    for over_x, over_z, both in spans:

        def round_rows(i, carry):
            T[i // (ns * nx), (i // nx) % ns, i % nx, both] = D[tab[3, i], both].astype(BF)
            return carry

        lax.fori_loop(0, nz * nx, round_rows, 0, unroll=8)
        stage.append((
            [
                lr.send(T.at[:, :, (x + d) % nx, over_x], RXA.at[d - 1, :, :, over_x], at(dx=d))
                for d in range(1, nx)
            ],
            [
                lr.send(T.at[q, :, :, over_z], RZB.at[e, :, :, over_z], at(dz=dz))
                for e, (q, dz) in enumerate(((zp, 1), (zm, -1)))
            ],
        ))

    for like, i in corner:
        lg.got(like, i, here)

    def mirror(s, carry):
        t = tab[0, s]
        p = G[lax.div(t, ns * nx), lax.rem(lax.div(t, nx), ns), lax.rem(t, nx)]
        M[s] = jnp.dot(p, B[s], preferred_element_type=F32) + M[tab[4, s]]
        return carry

    lax.fori_loop(0, slots, mirror, 0, unroll=UNROLL)

    def round_other(i, carry):
        MS[i] = M[tab[5, (1 - k) * ny + i]].astype(BF)
        return carry

    lax.fori_loop(0, ny, round_other, 0, unroll=8)
    swap = lm.send(MS, MR, at(dk=1))

    second = []

    def sums(p):
        over_x, over_z, _ = spans[p]
        for e in range(2):
            lr.got(RZB.at[e, :, :, over_z], stage[p][1][e], here)

        def sum_b(i, carry):
            s, w = i // nx, i % nx
            total = D[tab[3, (zr * ns + s) * nx + w], over_z]
            total = total + RZB[0, s, w, over_z].astype(F32) + RZB[1, s, w, over_z].astype(F32)
            SB[w, s, over_z] = total.astype(BF)
            return carry

        lax.fori_loop(0, ns * nx, sum_b, 0, unroll=4)
        to_x = [
            lr.send(SB.at[(x + d) % nx, :, over_z], RXB.at[d - 1, :, over_z], at(dx=d)) for d in range(1, nx)
        ]
        for d in range(1, nx):
            lr.got(RXA.at[d - 1, :, :, over_x], stage[p][0][d - 1], here)

        def sum_a(i, carry):
            q, s = i // ns, i % ns
            total = D[tab[3, i * nx + x], over_x]
            for d in range(1, nx):
                total = total + RXA[d - 1, q, s, over_x].astype(F32)
            SA[q, s, over_x] = total.astype(BF)
            return carry

        lax.fori_loop(0, NR * ns, sum_a, 0, unroll=4)
        to_z = [
            lr.send(SA.at[q, :, over_x], RZA.at[e, :, over_x], at(dz=dz))
            for e, (q, dz) in enumerate(((zp, 1), (zm, -1)))
        ]
        second.append((to_x, to_z))

    sums(0)

    lm.got(MR, swap, here)

    def sum_m(i, carry):
        N[i] = (M[tab[5, k * ny + i]] + MR[i].astype(F32)).astype(BF)
        return carry

    lax.fori_loop(0, ny, sum_m, 0, unroll=8)
    over_y = [lm.send(N.at[(y + d) % ny], YR.at[d - 1], at(dy=d)) for d in range(1, ny)]
    for p in range(1, len(spans)):
        sums(p)

    third = []
    for p, (over_x, over_z, both) in enumerate(spans):
        for e in range(2):
            lr.got(RZA.at[e, :, over_x], second[p][1][e], here)
        for d in range(1, nx):
            lr.got(RXB.at[d - 1, :, over_z], second[p][0][d - 1], here)
        for s in range(ns):
            a = SA[zr, s, over_x].astype(F32) + RZA[0, s, over_x].astype(F32) + RZA[1, s, over_x].astype(F32)
            b = SB[x, s, over_z].astype(F32)
            for d in range(1, nx):
                b = b + RXB[d - 1, s, over_z].astype(F32)
            S3[s, over_x] = a
            S3[s, over_z] = b
            SH[s, over_x] = a.astype(BF)
            SH[s, over_z] = b.astype(BF)
        third.append([
            lr.send(SH.at[place((zs + d) % ns), both], R3.at[d - 1, both], at(dz=NR * d)) for d in range(1, ns)
        ])

    total = M[tab[5, k * ny + y]] + MR[y].astype(F32)
    for d in range(1, ny):
        lm.got(YR.at[d - 1], over_y[d - 1], here)
        total = total + YR[d - 1].astype(F32)
    for cp in loads[4:]:
        cp.wait()
    mirrored = total.T
    scale = 2.0 / jnp.full((bs, bs), width[0], F32)
    for p, (_, _, both) in enumerate(spans):
        rows_of = slice(both.start, both.start + both.size)
        product = mirrored[rows_of] + S3[slot, both]
        product = product - center[0] * panel[both].astype(F32)
        for d in range(1, ns):
            lr.got(R3.at[d - 1, both], third[p][d - 1], here)
            product = product + R3[d - 1, both].astype(F32)
        out[both] = (scale[rows_of] * product - previous[both].astype(F32)).astype(BF)
    for lane in (ly, lg, lr, lm):
        lane.drain()


def body(nx, panel, previous, blocks, block_rows, block_cols, counts, center, half_width):
    bs = panel.shape[0]
    ny = lax.axis_size("row") // 2
    ns = lax.axis_size("col") // nx // NR
    slots = blocks.shape[2]
    hbm = pl.BlockSpec(memory_space=pltpu.HBM)
    dma = pltpu.SemaphoreType.DMA
    vmem = pltpu.VMEM
    gathers = (ns - 1) + min(ns, 3) * (nx + 1 + 4 * (nx - 1))
    reduces = len(PIECES) * (2 * (nx + 1) + ns - 1)
    return pl.pallas_call(
        functools.partial(kernel, nx, ny, ns),
        name="filter_step",
        out_shape=jax.ShapeDtypeStruct((bs, bs), BF),
        in_specs=[pl.BlockSpec(memory_space=pltpu.SMEM)] * 3 + [hbm] * 5,
        out_specs=pl.BlockSpec(memory_space=pltpu.VMEM),
        scratch_shapes=[
            vmem((bs, bs), BF),
            vmem((bs, bs), BF),
            vmem((slots, bs, bs), BF),
            vmem((1, slots), I32),
            vmem((1, slots), I32),
            vmem((8, 128), I32),
            pltpu.SMEM((8, 128), I32),
            vmem((2 * ny, bs, bs), BF),
            vmem((NR, ns, nx, bs, bs), BF),
            vmem((slots + 1, bs, bs), F32),
            vmem((slots + 1, bs, bs), F32),
            vmem((NR, ns, nx, bs, bs), BF),
            vmem((nx - 1, NR, ns, bs, bs), BF),
            vmem((2, ns, nx, bs, bs), BF),
            vmem((2, ns, bs, bs), BF),
            vmem((nx - 1, ns, bs, bs), BF),
            vmem((NR, ns, bs, bs), BF),
            vmem((nx, ns, bs, bs), BF),
            vmem((ns, bs, bs), F32),
            vmem((ns, bs, bs), BF),
            vmem((ns - 1, bs, bs), BF),
            vmem((ny, bs, bs), BF),
            vmem((ny, bs, bs), BF),
            vmem((ny, bs, bs), BF),
            vmem((ny - 1, bs, bs), BF),
            dma((6,)),
            dma((2 * ny - 1,)), dma((2 * ny - 1,)),
            dma((gathers,)), dma((gathers,)),
            dma((reduces,)), dma((reduces,)),
            dma((ny,)), dma((ny,)),
        ],
        compiler_params=pltpu.CompilerParams(
            collective_id=0, has_side_effects=True, vmem_limit_bytes=60 << 20
        ),
    )(
        counts, center, half_width, panel, previous, blocks.reshape(slots, bs, bs),
        block_rows.reshape(1, slots), block_cols.reshape(1, slots),
    )


def solution(mesh):
    placed = (
        P(("row", "col"), None),
        P(("row", "col"), None),
        P("row", "col", None, None, None),
        P("row", "col", None),
        P("row", "col", None),
        P("row", "col"),
        P(),
        P(),
    )
    return jax.shard_map(
        functools.partial(body, NX), mesh=mesh, in_specs=placed, out_specs=P(("row", "col"), None), check_vma=False
    )
```

```python
import functools

import jax
import jax.numpy as jnp
from jax import lax
from jax.experimental import pallas as pl
from jax.experimental.pallas import tpu as pltpu
from jax.sharding import PartitionSpec as P

MESH = pl.DeviceIdType.MESH
BF = jnp.bfloat16
F32 = jnp.float32
I32 = jnp.int32
NX = 4
NR = 3
GATHER_ROWS = 64
REDUCE_ROWS = 48
UNROLL = 32


class Lane:
    def __init__(self, sends, recvs):
        self.sends, self.recvs, self.count, self.started = sends, recvs, 0, []

    def make(self, src, dst, dev):
        i, self.count = self.count, self.count + 1
        cp = pltpu.make_async_remote_copy(
            src_ref=src, dst_ref=dst, send_sem=self.sends.at[i], recv_sem=self.recvs.at[i],
            device_id=dev, device_id_type=MESH,
        )
        self.started.append(cp)
        return i, cp

    def send(self, src, dst, dev):
        i, cp = self.make(src, dst, dev)
        cp.start()
        return i

    def got(self, like, i, dev):
        pltpu.make_async_remote_copy(
            src_ref=like, dst_ref=like, send_sem=self.recvs.at[i], recv_sem=self.recvs.at[i],
            device_id=dev, device_id_type=MESH,
        ).wait_recv()

    def drain(self):
        for cp in self.started:
            cp.wait_send()


def kernel(nx, ny, ns, count, center, width, panel_hbm, previous_hbm, blocks_hbm, rows_hbm, cols_hbm, out,
           panel, previous, B, rows, cols, tabv, tab,
           C, G, D, M, T, RXA, RZB, RZA, RXB, SA, SB, S3, SH, R3, MS, MR, N, YR,
           lsem, cs, cr, gs, gr, rs, rr, ms, mr):
    row = lax.axis_index("row")
    col = lax.axis_index("col")
    y, k = row // 2, row % 2
    z, x = col // nx, col % nx
    zs, zr = z // NR, z % NR
    nz = ns * NR
    h = ns // 2
    par, pair = zs % 2, zs // 2
    slot = par * h + pair
    slots = B.shape[0]
    bs = panel.shape[0]
    zm, zp = (zr + NR - 1) % NR, (zr + 1) % NR
    ga, ra = GATHER_ROWS, REDUCE_ROWS
    lo, hi = pl.ds(0, ga), pl.ds(ga, bs - ga)
    rlo, rhi = pl.ds(0, ra), pl.ds(ra, bs - ra)
    ly, lg, lr, lm = Lane(cs, cr), Lane(gs, gr), Lane(rs, rr), Lane(ms, mr)

    def at(dy=0, dk=0, dz=0, dx=0):
        return {
            "row": ((y + dy) % ny) * 2 + (k + dk) % 2,
            "col": ((z + dz) % nz) * nx + (x + dx) % nx,
        }

    here = at()
    loads = [
        pltpu.make_async_copy(a, b, lsem.at[i])
        for i, (a, b) in enumerate([
            (panel_hbm, panel), (rows_hbm, rows), (cols_hbm, cols), (blocks_hbm, B), (previous_hbm, previous),
        ])
    ]
    loads[0].start()
    peers = [at(dk=1)]
    peers += [at(dy=d) for d in range(1, ny)]
    peers += [at(dz=NR * d) for d in range(1, ns)]
    peers += [at(dz=1), at(dz=-1)]
    peers += [at(dx=d) for d in range(1, nx)]
    barrier = pltpu.get_barrier_semaphore()
    for dev in peers:
        pl.semaphore_signal(barrier, inc=1, device_id=dev, device_id_type=MESH)
    for cp in loads[1:]:
        cp.start()
    loads[0].wait()
    own = panel[...]
    mine = C.at[k * ny + y]
    C[k * ny + y] = own
    G[zr, slot, x] = own.astype(F32).T.astype(BF)
    pl.semaphore_wait(barrier, len(peers))

    ownt = G.at[zr, slot, x]
    first = {d: lg.send(ownt, ownt, at(dz=NR * d)) for d in range(1, ns, 2)}
    for d in range(1, ny):
        ly.send(mine, mine, at(dy=d))
    ly.send(mine, mine, at(dk=1))

    def spread(piece):
        return (
            [lg.send(piece, piece, at(dz=dz)) for dz in (1, -1)],
            [lg.send(piece, piece, at(dx=d)) for d in range(1, nx)],
        )

    near = [spread(ownt)]
    first.update({d: lg.send(ownt, ownt, at(dz=NR * d)) for d in range(2, ns, 2)})

    D[slots] = jnp.zeros(D.shape[1:], F32)
    M[slots] = jnp.zeros(M.shape[1:], F32)
    tabv[...] = jnp.zeros(tabv.shape, I32)
    for cp in loads[1:3]:
        cp.wait()
    shift = nx.bit_length() - 1
    r = rows[...]
    rz = lax.shift_right_logical(r, shift)
    rzs = lax.shift_right_logical(rz * 11, 5)
    rk = (rz - rzs * NR) * ns + (rzs & 1) * h + lax.shift_right_logical(rzs, 1)
    rk = rk * nx + (r & (nx - 1))
    c = cols[...]
    ck = (c & 1) * ny + lax.shift_right_logical(c, 1)
    square = (slots, slots)
    t_of = lax.broadcasted_iota(I32, square, 0)
    s_of = lax.broadcasted_iota(I32, square, 1)
    alive = t_of < count[0, 0]
    tabv[0:1, 0:slots] = rk
    tabv[1:2, 0:slots] = ck
    for i, key in ((2, rk), (4, ck)):
        wide = jnp.broadcast_to(key, square)
        tall = wide.T
        before = jnp.max(jnp.where((tall == wide) & (t_of < s_of), t_of, -1), axis=0, keepdims=True)
        last = jnp.max(jnp.where((tall == s_of) & alive, t_of, -1), axis=0, keepdims=True)
        tabv[i : i + 1, 0:slots] = jnp.where(before < 0, slots, before)
        tabv[i + 1 : i + 2, 0:slots] = jnp.where(last < 0, slots, last)
    table_copy = pltpu.make_async_copy(tabv, tab, lsem.at[5])
    table_copy.start()

    for d in range(1, ns, 2):
        lg.got(ownt, first[d], here)
    near.append(spread(G.at[zr, pl.ds((1 - par) * h, h), x]))

    def slots_of(source, kind):
        szs = source // NR
        spar, spair = szs % 2, szs // 2
        start = (spar * h + spair, (1 - spar) * h, spar * h + 1 - spair)[kind]
        return pl.ds(start, h if kind == 1 else 1)

    corner = []

    def corners(kind):
        like = G.at[zr, slots_of(z, kind), x]
        for e, dz in enumerate((1, -1)):
            lg.got(like, near[kind][0][e], here)
            source = (z + nz - dz) % nz
            part = G.at[source % NR, slots_of(source, kind), x, lo]
            for d in range(1, nx):
                corner.append((part, lg.send(part, part, at(dx=d))))
        for d in range(1, nx):
            lg.got(like, near[kind][1][d - 1], here)
            part = G.at[zr, slots_of(z, kind), (x + nx - d) % nx, hi]
            for dz in (1, -1):
                corner.append((part, lg.send(part, part, at(dz=dz))))

    corners(0)
    if ns > 2:
        for d in range(2, ns, 2):
            lg.got(ownt, first[d], here)
        near.append(spread(G.at[zr, slots_of(z, 2), x]))

    for d in range(1, ny):
        ly.got(mine, d - 1, here)
        there = C.at[k * ny + (y + ny - d) % ny]
        ly.send(there, there, at(dk=1))
    corners(1)

    table_copy.wait()
    loads[3].wait()
    for i in range(ny - 1, 2 * ny - 1):
        ly.got(mine, i, here)

    def direct(s, carry):
        D[s] = jnp.dot(B[s], C[tab[1, s]], preferred_element_type=F32) + D[tab[2, s]]
        return carry

    lax.fori_loop(0, slots, direct, 0, unroll=UNROLL)

    def round_rows(i, carry):
        T[i // (ns * nx), (i // nx) % ns, i % nx] = D[tab[3, i]].astype(BF)
        return carry

    lax.fori_loop(0, nz * nx, round_rows, 0, unroll=8)
    if ns > 2:
        corners(2)
    stage = []
    for p in range(2):
        part = pl.ds(p * h, h)
        stage.append((
            [lr.send(T.at[:, part, (x + d) % nx, rlo], RXA.at[d - 1, :, part], at(dx=d)) for d in range(1, nx)],
            [
                lr.send(T.at[q, part, :, rhi], RZB.at[e, part], at(dz=dz))
                for e, (q, dz) in enumerate(((zp, 1), (zm, -1)))
            ],
        ))

    for like, i in corner:
        lg.got(like, i, here)

    def mirror(s, carry):
        t = tab[0, s]
        p = G[lax.div(t, ns * nx), lax.rem(lax.div(t, nx), ns), lax.rem(t, nx)]
        M[s] = jnp.dot(p, B[s], preferred_element_type=F32) + M[tab[4, s]]
        return carry

    lax.fori_loop(0, slots, mirror, 0, unroll=UNROLL)

    other = (pl.ds(0, ny // 2), pl.ds(ny // 2, ny - ny // 2))

    def round_other(i, carry):
        MS[i] = M[tab[5, (1 - k) * ny + lax.rem(y + i + 1, ny)]].astype(BF)
        return carry

    swap = []
    for part in other:
        lax.fori_loop(part.start, part.start + part.size, round_other, 0, unroll=part.size)
        swap.append(lm.send(MS.at[part], MR.at[part], at(dk=1)))

    second = []

    def sums(p):
        part = pl.ds(p * h, h)
        for e in range(2):
            lr.got(RZB.at[e, part], stage[p][1][e], here)

        def sum_b(i, carry):
            s, w = p * h + i // nx, i % nx
            total = D[tab[3, (zr * ns + s) * nx + w]][ra:]
            total = total + RZB[0, s, w].astype(F32) + RZB[1, s, w].astype(F32)
            SB[w, s] = total.astype(BF)
            return carry

        lax.fori_loop(0, h * nx, sum_b, 0, unroll=4)
        over_x = [lr.send(SB.at[(x + d) % nx, part], RXB.at[d - 1, part], at(dx=d)) for d in range(1, nx)]
        for d in range(1, nx):
            lr.got(RXA.at[d - 1, :, part], stage[p][0][d - 1], here)

        def sum_a(i, carry):
            q, s = i // h, p * h + i % h
            total = D[tab[3, (q * ns + s) * nx + x]][:ra]
            for d in range(1, nx):
                total = total + RXA[d - 1, q, s].astype(F32)
            SA[q, s] = total.astype(BF)
            return carry

        lax.fori_loop(0, NR * h, sum_a, 0, unroll=NR)
        over_z = [
            lr.send(SA.at[q, part], RZA.at[e, part], at(dz=dz)) for e, (q, dz) in enumerate(((zp, 1), (zm, -1)))
        ]
        second.append((over_x, over_z))

    def sum_m(i, carry):
        N[i] = (M[tab[5, k * ny + lax.rem(y + i + 1, ny)]] + MR[i].astype(F32)).astype(BF)
        return carry

    over_y = []
    for part, i in zip(other, swap):
        lm.got(MR.at[part], i, here)
        lax.fori_loop(part.start, part.start + part.size, sum_m, 0, unroll=part.size)
        for d in range(part.start + 1, min(part.start + part.size, ny - 1) + 1):
            over_y.append(lm.send(N.at[d - 1], YR.at[d - 1], at(dy=d)))
    sums(0)
    sums(1)

    third = []
    for d in range(1, ns):
        to = (zs + d) % ns
        third.append((to, *lr.make(SH.at[(to % 2) * h + to // 2], R3.at[d - 1], at(dz=NR * d))))
    for p in range(2):
        part = pl.ds(p * h, h)
        over_x, over_z = second[p]
        for e in range(2):
            lr.got(RZA.at[e, part], over_z[e], here)
        for d in range(1, nx):
            lr.got(RXB.at[d - 1, part], over_x[d - 1], here)
        for j in range(h):
            s = p * h + j
            a = SA[zr, s].astype(F32) + RZA[0, s].astype(F32) + RZA[1, s].astype(F32)
            b = SB[x, s].astype(F32)
            for d in range(1, nx):
                b = b + RXB[d - 1, s].astype(F32)
            S3[s, :ra] = a
            S3[s, ra:] = b
            SH[s, :ra] = a.astype(BF)
            SH[s, ra:] = b.astype(BF)
        for to, _, cp in third:
            pl.when(to % 2 == p)(cp.start)

    total = M[tab[5, k * ny + y]] + MR[ny - 1].astype(F32)
    for d in range(1, ny):
        lm.got(YR.at[d - 1], over_y[d - 1], here)
        total = total + YR[d - 1].astype(F32)
    for cp in loads[4:]:
        cp.wait()
    product = total.T + S3[slot]
    scale = 2.0 / jnp.full((bs, bs), width[0], F32)
    moved = center[0] * panel[...].astype(F32)
    before = previous[...].astype(F32)
    for d in range(1, ns):
        lr.got(R3.at[d - 1], third[d - 1][1], here)
        product = product + R3[d - 1].astype(F32)
    out[...] = (scale * (product - moved) - before).astype(BF)
    for lane in (ly, lg, lr, lm):
        lane.drain()


def body(nx, panel, previous, blocks, block_rows, block_cols, counts, center, half_width):
    bs = panel.shape[0]
    ny = lax.axis_size("row") // 2
    ns = lax.axis_size("col") // nx // NR
    slots = blocks.shape[2]
    ra, rb = REDUCE_ROWS, bs - REDUCE_ROWS
    hbm = pl.BlockSpec(memory_space=pltpu.HBM)
    dma = pltpu.SemaphoreType.DMA
    vmem = pltpu.VMEM
    gathers = (ns - 1) + min(ns, 3) * (nx + 1 + 4 * (nx - 1))
    reduces = 4 * (nx + 1) + ns - 1
    return pl.pallas_call(
        functools.partial(kernel, nx, ny, ns),
        name="filter_step",
        out_shape=jax.ShapeDtypeStruct((bs, bs), BF),
        in_specs=[pl.BlockSpec(memory_space=pltpu.SMEM)] * 3 + [hbm] * 5,
        out_specs=pl.BlockSpec(memory_space=pltpu.VMEM),
        scratch_shapes=[
            vmem((bs, bs), BF),
            vmem((bs, bs), BF),
            vmem((slots, bs, bs), BF),
            vmem((1, slots), I32),
            vmem((1, slots), I32),
            vmem((8, 128), I32),
            pltpu.SMEM((8, 128), I32),
            vmem((2 * ny, bs, bs), BF),
            vmem((NR, ns, nx, bs, bs), BF),
            vmem((slots + 1, bs, bs), F32),
            vmem((slots + 1, bs, bs), F32),
            vmem((NR, ns, nx, bs, bs), BF),
            vmem((nx - 1, NR, ns, ra, bs), BF),
            vmem((2, ns, nx, rb, bs), BF),
            vmem((2, ns, ra, bs), BF),
            vmem((nx - 1, ns, rb, bs), BF),
            vmem((NR, ns, ra, bs), BF),
            vmem((nx, ns, rb, bs), BF),
            vmem((ns, bs, bs), F32),
            vmem((ns, bs, bs), BF),
            vmem((ns - 1, bs, bs), BF),
            vmem((ny, bs, bs), BF),
            vmem((ny, bs, bs), BF),
            vmem((ny, bs, bs), BF),
            vmem((ny - 1, bs, bs), BF),
            dma((6,)),
            dma((2 * ny - 1,)), dma((2 * ny - 1,)),
            dma((gathers,)), dma((gathers,)),
            dma((reduces,)), dma((reduces,)),
            dma((ny + 1,)), dma((ny + 1,)),
        ],
        compiler_params=pltpu.CompilerParams(
            collective_id=0, has_side_effects=True, vmem_limit_bytes=60 << 20
        ),
    )(
        counts, center, half_width, panel, previous, blocks.reshape(slots, bs, bs),
        block_rows.reshape(1, slots), block_cols.reshape(1, slots),
    )


def solution(mesh):
    placed = (
        P(("row", "col"), None),
        P(("row", "col"), None),
        P("row", "col", None, None, None),
        P("row", "col", None),
        P("row", "col", None),
        P("row", "col"),
        P(),
        P(),
    )
    return jax.shard_map(
        functools.partial(body, NX), mesh=mesh, in_specs=placed, out_specs=P(("row", "col"), None), check_vma=False
    )
```

```python
import functools

import jax
import jax.numpy as jnp
from jax import lax
from jax.experimental import pallas as pl
from jax.experimental.pallas import tpu as pltpu
from jax.sharding import PartitionSpec as P

MESH = pl.DeviceIdType.MESH
BF = jnp.bfloat16
F32 = jnp.float32
I32 = jnp.int32
NX = 4
NR = 3
GATHER_ROWS = 64
REDUCE_ROWS = 48
UNROLL = 32


class Lane:
    def __init__(self, sends, recvs):
        self.sends, self.recvs, self.count, self.started = sends, recvs, 0, []

    def make(self, src, dst, dev):
        i, self.count = self.count, self.count + 1
        cp = pltpu.make_async_remote_copy(
            src_ref=src, dst_ref=dst, send_sem=self.sends.at[i], recv_sem=self.recvs.at[i],
            device_id=dev, device_id_type=MESH,
        )
        self.started.append(cp)
        return i, cp

    def send(self, src, dst, dev):
        i, cp = self.make(src, dst, dev)
        cp.start()
        return i

    def got(self, like, i, dev):
        pltpu.make_async_remote_copy(
            src_ref=like, dst_ref=like, send_sem=self.recvs.at[i], recv_sem=self.recvs.at[i],
            device_id=dev, device_id_type=MESH,
        ).wait_recv()

    def drain(self):
        for cp in self.started:
            cp.wait_send()


def kernel(nx, ny, ns, count, center, width, panel_hbm, previous_hbm, blocks_hbm, rows_hbm, cols_hbm, out,
           panel, previous, B, rows, cols, tabv, tab,
           C, G, D, M, T, RXA, RZB, RZA, RXB, SA, SB, S3, SH, R3, MS, MR, N, YR,
           lsem, cs, cr, gs, gr, rs, rr, ms, mr):
    row = lax.axis_index("row")
    col = lax.axis_index("col")
    y, k = row // 2, row % 2
    z, x = col // nx, col % nx
    zs, zr = z // NR, z % NR
    nz = ns * NR
    h = ns // 2
    par, pair = zs % 2, zs // 2
    slot = par * h + pair
    slots = B.shape[0]
    bs = panel.shape[0]
    zm, zp = (zr + NR - 1) % NR, (zr + 1) % NR
    ga, ra = GATHER_ROWS, REDUCE_ROWS
    lo, hi = pl.ds(0, ga), pl.ds(ga, bs - ga)
    rlo, rhi = pl.ds(0, ra), pl.ds(ra, bs - ra)
    ly, lg, lr, lm = Lane(cs, cr), Lane(gs, gr), Lane(rs, rr), Lane(ms, mr)

    def at(dy=0, dk=0, dz=0, dx=0):
        return {
            "row": ((y + dy) % ny) * 2 + (k + dk) % 2,
            "col": ((z + dz) % nz) * nx + (x + dx) % nx,
        }

    here = at()

    def nearest(n):
        return sorted(range(1, n), key=lambda d: min(d, n - d))

    near_x, near_y = nearest(nx), nearest(ny)
    far_x, far_y = near_x[::-1], near_y[::-1]
    loads = [
        pltpu.make_async_copy(a, b, lsem.at[i])
        for i, (a, b) in enumerate([
            (panel_hbm, panel), (rows_hbm, rows), (cols_hbm, cols), (blocks_hbm, B), (previous_hbm, previous),
        ])
    ]
    loads[0].start()
    peers = [at(dk=1)]
    peers += [at(dy=d) for d in range(1, ny)]
    peers += [at(dz=NR * d) for d in range(1, ns)]
    peers += [at(dz=1), at(dz=-1)]
    peers += [at(dx=d) for d in range(1, nx)]
    barrier = pltpu.get_barrier_semaphore()
    for dev in peers:
        pl.semaphore_signal(barrier, inc=1, device_id=dev, device_id_type=MESH)
    for cp in loads[1:]:
        cp.start()
    loads[0].wait()
    own = panel[...]
    mine = C.at[k * ny + y]
    C[k * ny + y] = own
    G[zr, slot, x] = own.astype(F32).T.astype(BF)
    pl.semaphore_wait(barrier, len(peers))

    ownt = G.at[zr, slot, x]
    first = {d: lg.send(ownt, ownt, at(dz=NR * d)) for d in range(1, ns, 2)}
    along_y = {d: ly.send(mine, mine, at(dy=d)) for d in far_y}
    across = [ly.send(mine, mine, at(dk=1))]

    def spread(piece):
        return (
            [lg.send(piece, piece, at(dz=dz)) for dz in (1, -1)],
            {d: lg.send(piece, piece, at(dx=d)) for d in far_x},
        )

    near = [spread(ownt)]
    first.update({d: lg.send(ownt, ownt, at(dz=NR * d)) for d in range(2, ns, 2)})

    D[slots] = jnp.zeros(D.shape[1:], F32)
    M[slots] = jnp.zeros(M.shape[1:], F32)
    tabv[...] = jnp.zeros(tabv.shape, I32)
    for cp in loads[1:3]:
        cp.wait()
    shift = nx.bit_length() - 1
    r = rows[...]
    rz = lax.shift_right_logical(r, shift)
    rzs = lax.shift_right_logical(rz * 11, 5)
    rk = (rz - rzs * NR) * ns + (rzs & 1) * h + lax.shift_right_logical(rzs, 1)
    rk = rk * nx + (r & (nx - 1))
    c = cols[...]
    ck = (c & 1) * ny + lax.shift_right_logical(c, 1)
    square = (slots, slots)
    t_of = lax.broadcasted_iota(I32, square, 0)
    s_of = lax.broadcasted_iota(I32, square, 1)
    alive = t_of < count[0, 0]
    tabv[0:1, 0:slots] = rk
    tabv[1:2, 0:slots] = ck
    for i, key in ((2, rk), (4, ck)):
        wide = jnp.broadcast_to(key, square)
        tall = wide.T
        before = jnp.max(jnp.where((tall == wide) & (t_of < s_of), t_of, -1), axis=0, keepdims=True)
        last = jnp.max(jnp.where((tall == s_of) & alive, t_of, -1), axis=0, keepdims=True)
        tabv[i : i + 1, 0:slots] = jnp.where(before < 0, slots, before)
        tabv[i + 1 : i + 2, 0:slots] = jnp.where(last < 0, slots, last)
    table_copy = pltpu.make_async_copy(tabv, tab, lsem.at[5])
    table_copy.start()

    for d in range(1, ns, 2):
        lg.got(ownt, first[d], here)
    near.append(spread(G.at[zr, pl.ds((1 - par) * h, h), x]))

    def slots_of(source, kind):
        szs = source // NR
        spar, spair = szs % 2, szs // 2
        start = (spar * h + spair, (1 - spar) * h, spar * h + 1 - spair)[kind]
        return pl.ds(start, h if kind == 1 else 1)

    corner = []

    def corners(kind):
        like = G.at[zr, slots_of(z, kind), x]
        for e, dz in enumerate((1, -1)):
            lg.got(like, near[kind][0][e], here)
            source = (z + nz - dz) % nz
            part = G.at[source % NR, slots_of(source, kind), x, lo]
            for d in far_x:
                corner.append((part, lg.send(part, part, at(dx=d))))
        for d in near_x:
            lg.got(like, near[kind][1][d], here)
            part = G.at[zr, slots_of(z, kind), (x + nx - d) % nx, hi]
            for dz in (1, -1):
                corner.append((part, lg.send(part, part, at(dz=dz))))

    corners(0)
    if ns > 2:
        for d in range(2, ns, 2):
            lg.got(ownt, first[d], here)
        near.append(spread(G.at[zr, slots_of(z, 2), x]))

    for d in near_y:
        ly.got(mine, along_y[d], here)
        there = C.at[k * ny + (y + ny - d) % ny]
        across.append(ly.send(there, there, at(dk=1)))
    corners(1)

    table_copy.wait()
    loads[3].wait()
    for i in across:
        ly.got(mine, i, here)

    def direct(s, carry):
        D[s] = jnp.dot(B[s], C[tab[1, s]], preferred_element_type=F32) + D[tab[2, s]]
        return carry

    lax.fori_loop(0, slots, direct, 0, unroll=UNROLL)

    def round_rows(i, carry):
        T[i // (ns * nx), (i // nx) % ns, i % nx] = D[tab[3, i]].astype(BF)
        return carry

    lax.fori_loop(0, nz * nx, round_rows, 0, unroll=8)
    if ns > 2:
        corners(2)
    stage = []
    for p in range(2):
        part = pl.ds(p * h, h)
        stage.append((
            {d: lr.send(T.at[:, part, (x + d) % nx, rlo], RXA.at[d - 1, :, part], at(dx=d)) for d in far_x},
            [
                lr.send(T.at[q, part, :, rhi], RZB.at[e, part], at(dz=dz))
                for e, (q, dz) in enumerate(((zp, 1), (zm, -1)))
            ],
        ))

    for like, i in corner:
        lg.got(like, i, here)

    def mirror(s, carry):
        t = tab[0, s]
        p = G[lax.div(t, ns * nx), lax.rem(lax.div(t, nx), ns), lax.rem(t, nx)]
        M[s] = jnp.dot(p, B[s], preferred_element_type=F32) + M[tab[4, s]]
        return carry

    lax.fori_loop(0, slots, mirror, 0, unroll=UNROLL)

    other = (pl.ds(0, ny // 2), pl.ds(ny // 2, ny - ny // 2))

    def round_other(i, carry):
        MS[i] = M[tab[5, (1 - k) * ny + lax.rem(y + i + 1, ny)]].astype(BF)
        return carry

    swap = []
    for part in other:
        lax.fori_loop(part.start, part.start + part.size, round_other, 0, unroll=part.size)
        swap.append(lm.send(MS.at[part], MR.at[part], at(dk=1)))

    second = []

    def sums(p):
        part = pl.ds(p * h, h)
        for e in range(2):
            lr.got(RZB.at[e, part], stage[p][1][e], here)

        def sum_b(i, carry):
            s, w = p * h + i // nx, i % nx
            total = D[tab[3, (zr * ns + s) * nx + w]][ra:]
            total = total + RZB[0, s, w].astype(F32) + RZB[1, s, w].astype(F32)
            SB[w, s] = total.astype(BF)
            return carry

        lax.fori_loop(0, h * nx, sum_b, 0, unroll=4)
        over_x = {d: lr.send(SB.at[(x + d) % nx, part], RXB.at[d - 1, part], at(dx=d)) for d in far_x}
        for d in range(1, nx):
            lr.got(RXA.at[d - 1, :, part], stage[p][0][d], here)

        def sum_a(i, carry):
            q, s = i // h, p * h + i % h
            total = D[tab[3, (q * ns + s) * nx + x]][:ra]
            for d in range(1, nx):
                total = total + RXA[d - 1, q, s].astype(F32)
            SA[q, s] = total.astype(BF)
            return carry

        lax.fori_loop(0, NR * h, sum_a, 0, unroll=NR)
        over_z = [
            lr.send(SA.at[q, part], RZA.at[e, part], at(dz=dz)) for e, (q, dz) in enumerate(((zp, 1), (zm, -1)))
        ]
        second.append((over_x, over_z))

    def sum_m(i, carry):
        N[i] = (M[tab[5, k * ny + lax.rem(y + i + 1, ny)]] + MR[i].astype(F32)).astype(BF)
        return carry

    over_y = {}
    for part, i in zip(other, swap):
        lm.got(MR.at[part], i, here)
        lax.fori_loop(part.start, part.start + part.size, sum_m, 0, unroll=part.size)
        for d in far_y:
            if part.start < d <= part.start + part.size:
                over_y[d] = lm.send(N.at[d - 1], YR.at[d - 1], at(dy=d))
    sums(0)
    sums(1)

    third = []
    for d in range(1, ns):
        to = (zs + d) % ns
        third.append((to, *lr.make(SH.at[(to % 2) * h + to // 2], R3.at[d - 1], at(dz=NR * d))))
    for p in range(2):
        part = pl.ds(p * h, h)
        over_x, over_z = second[p]
        for e in range(2):
            lr.got(RZA.at[e, part], over_z[e], here)
        for d in range(1, nx):
            lr.got(RXB.at[d - 1, part], over_x[d], here)
        for j in range(h):
            s = p * h + j
            a = SA[zr, s].astype(F32) + RZA[0, s].astype(F32) + RZA[1, s].astype(F32)
            b = SB[x, s].astype(F32)
            for d in range(1, nx):
                b = b + RXB[d - 1, s].astype(F32)
            S3[s, :ra] = a
            S3[s, ra:] = b
            SH[s, :ra] = a.astype(BF)
            SH[s, ra:] = b.astype(BF)
        for to, _, cp in third:
            pl.when(to % 2 == p)(cp.start)

    total = M[tab[5, k * ny + y]] + MR[ny - 1].astype(F32)
    for d in range(1, ny):
        lm.got(YR.at[d - 1], over_y[d], here)
        total = total + YR[d - 1].astype(F32)
    for cp in loads[4:]:
        cp.wait()
    product = total.T + S3[slot]
    scale = 2.0 / jnp.full((bs, bs), width[0], F32)
    moved = center[0] * panel[...].astype(F32)
    before = previous[...].astype(F32)
    for d in range(1, ns):
        lr.got(R3.at[d - 1], third[d - 1][1], here)
        product = product + R3[d - 1].astype(F32)
    out[...] = (scale * (product - moved) - before).astype(BF)
    for lane in (ly, lg, lr, lm):
        lane.drain()


def body(nx, panel, previous, blocks, block_rows, block_cols, counts, center, half_width):
    bs = panel.shape[0]
    ny = lax.axis_size("row") // 2
    ns = lax.axis_size("col") // nx // NR
    slots = blocks.shape[2]
    ra, rb = REDUCE_ROWS, bs - REDUCE_ROWS
    hbm = pl.BlockSpec(memory_space=pltpu.HBM)
    dma = pltpu.SemaphoreType.DMA
    vmem = pltpu.VMEM
    gathers = (ns - 1) + min(ns, 3) * (nx + 1 + 4 * (nx - 1))
    reduces = 4 * (nx + 1) + ns - 1
    return pl.pallas_call(
        functools.partial(kernel, nx, ny, ns),
        name="filter_step",
        out_shape=jax.ShapeDtypeStruct((bs, bs), BF),
        in_specs=[pl.BlockSpec(memory_space=pltpu.SMEM)] * 3 + [hbm] * 5,
        out_specs=pl.BlockSpec(memory_space=pltpu.VMEM),
        scratch_shapes=[
            vmem((bs, bs), BF),
            vmem((bs, bs), BF),
            vmem((slots, bs, bs), BF),
            vmem((1, slots), I32),
            vmem((1, slots), I32),
            vmem((8, 128), I32),
            pltpu.SMEM((8, 128), I32),
            vmem((2 * ny, bs, bs), BF),
            vmem((NR, ns, nx, bs, bs), BF),
            vmem((slots + 1, bs, bs), F32),
            vmem((slots + 1, bs, bs), F32),
            vmem((NR, ns, nx, bs, bs), BF),
            vmem((nx - 1, NR, ns, ra, bs), BF),
            vmem((2, ns, nx, rb, bs), BF),
            vmem((2, ns, ra, bs), BF),
            vmem((nx - 1, ns, rb, bs), BF),
            vmem((NR, ns, ra, bs), BF),
            vmem((nx, ns, rb, bs), BF),
            vmem((ns, bs, bs), F32),
            vmem((ns, bs, bs), BF),
            vmem((ns - 1, bs, bs), BF),
            vmem((ny, bs, bs), BF),
            vmem((ny, bs, bs), BF),
            vmem((ny, bs, bs), BF),
            vmem((ny - 1, bs, bs), BF),
            dma((6,)),
            dma((2 * ny - 1,)), dma((2 * ny - 1,)),
            dma((gathers,)), dma((gathers,)),
            dma((reduces,)), dma((reduces,)),
            dma((ny + 1,)), dma((ny + 1,)),
        ],
        compiler_params=pltpu.CompilerParams(
            collective_id=0, has_side_effects=True, vmem_limit_bytes=60 << 20
        ),
    )(
        counts, center, half_width, panel, previous, blocks.reshape(slots, bs, bs),
        block_rows.reshape(1, slots), block_cols.reshape(1, slots),
    )


def solution(mesh):
    placed = (
        P(("row", "col"), None),
        P(("row", "col"), None),
        P("row", "col", None, None, None),
        P("row", "col", None),
        P("row", "col", None),
        P("row", "col"),
        P(),
        P(),
    )
    return jax.shard_map(
        functools.partial(body, NX), mesh=mesh, in_specs=placed, out_specs=P(("row", "col"), None), check_vma=False
    )
```
